32 devices in a mesh: groups: 2 (over x), chan: 16 (over z, y, core), freq: 1.
Axes of the slice: x: 2, y: 2, z: 4, core: 2. Of those that a mesh axis runs over, the one named last changes fastest.
Arguments:
- raw: bfloat16 [256, 16, 12000], P(('groups', 'chan'), 'freq'), parts along dimension 0, may hold values from -100 to 100, as said below
- lengths: int32 [256, 16], P(('groups', 'chan'), 'freq'), parts along dimension 0, may hold values from 6000 to 12000
- quality: int32 [256], P('groups'), parts along dimension 0, may hold values 0 or 1
- assignment: int32 [256], P('groups'), parts along dimension 0, may hold values from 0 to 127, as said below
Outputs:
- cross: bfloat16 [512, 256, 2, 128], P('freq', ('groups', 'chan')), parts along dimension 1
The draws below stay inside these ranges and needn't reach their ends.
There are 2 independent parts, one for each index of `groups`. The reference program is written for one: setup_inputs(seed, part) draws one part's arguments, and reference() takes and returns one part's arrays. A program takes and returns all parts, laid end to end along the dimension named above; each array names one. Nothing has to cross between parts.
Inputs may be any that keep to these rules, and one draw needn't show every extreme that they name: `raw`: records are clipped to this range. `assignment`: A permutation. The 8 channels of one file block (consecutive entries) land at most 1 in any one block of 8 consecutive positions, and some pair of blocks reaches 1.
All inputs are finite; a program needn't handle non-finite values.
Results may differ from the reference program's by a relative error of at most 0.012.
The reference program's roundings to bfloat16 on the way count: a program that leaves them out, or rounds other values in their place, can miss the bound.
Values may be sent and summed in bfloat16 or wider, within the bound.
A program may use at most 128 MiB of HBM per device.

```python
import math
import jax
import jax.numpy as jnp
from jax import lax

CH_BLK = 8
W = 16
WIN = 12000
NB = 512
K0 = 6
SUB = 32
CH = 128
CAP = 1


def draw_raw(key, part):
    keys = jax.random.split(jax.random.fold_in(key, 11), 5)
    samples = jnp.arange(WIN, dtype=jnp.int32)
    spread = math.log(10.0)
    values = jax.random.truncated_normal(keys[1], -4.0, 4.0, (CH, W, WIN), jnp.float32)
    scales = jnp.exp(jax.random.uniform(keys[0], (CH, 1, 1), jnp.float32) * spread)
    tone_bins = jax.random.randint(keys[2], (CH, 6), K0, K0 + NB)
    tone_sizes = jnp.exp(jax.random.uniform(keys[3], (CH, 6), jnp.float32, math.log(0.5), math.log(5.0)))
    phases = jax.random.uniform(keys[4], (CH, W, 6), jnp.float32, 0.0, 2.0 * math.pi)
    for number in range(6):
        residue = tone_bins[:, number, None, None] * samples[None, None, :] % WIN
        angles = residue.astype(jnp.float32) * (2.0 * math.pi / WIN) + phases[:, :, number, None]
        values = values + tone_sizes[:, number, None, None] * jnp.cos(angles)
    return jnp.clip(scales * values, -100.0, 100.0).astype(jnp.bfloat16)


def draw_assignment(key, part):
    keys = jax.random.split(jax.random.fold_in(key, 23), 4)
    groups_count = CH // CH_BLK
    offsets = jax.random.permutation(keys[0], groups_count * CAP)[:CH_BLK] // CAP
    source_order = jax.random.permutation(keys[1], groups_count)
    target_order = jax.random.permutation(keys[2], groups_count)
    arrival = jax.vmap(lambda subkey: jax.random.permutation(subkey, CH_BLK))(jax.random.split(keys[3], groups_count))
    targets = target_order[(source_order[:, None] + offsets[None, :]) % groups_count]
    row_numbers = jnp.broadcast_to(jnp.arange(CH_BLK, dtype=jnp.int32)[None, :], targets.shape)
    return (targets * CH_BLK + arrival[targets, row_numbers]).reshape(CH).astype(jnp.int32)


def place_ends(result, own_key, low, top_value):
    longest = result.shape.index(max(result.shape))
    spots = []
    for shift in (0, 1):
        where = [jax.random.randint(jax.random.fold_in(own_key, axis), (), 0, length) for axis, length in enumerate(result.shape)]
        where[longest] = (where[longest] + shift) % result.shape[longest]
        spots.append(tuple(where))
    return result.at[spots[0]].set(low).at[spots[1]].set(top_value)


def setup_inputs(seed: int = 0, part: int = 0) -> dict:
    splits = jax.random.split(jax.random.key(seed), 5)
    part_keys = jax.random.split(jax.random.fold_in(splits[4], part), 5)
    return {
        "raw": draw_raw(jax.random.fold_in(jax.random.fold_in(splits[4], part), 71), part),
        "lengths": place_ends(jax.random.randint(part_keys[1], (CH, W), WIN // 2, WIN + 1), jax.random.fold_in(part_keys[1], 1), WIN // 2, WIN).astype(jnp.int32),
        "quality": place_ends((jax.random.randint(part_keys[2], (CH,), 0, 8) < 7).astype(jnp.int32), jax.random.fold_in(part_keys[2], 1), 0, 1),
        "assignment": draw_assignment(jax.random.fold_in(jax.random.fold_in(splits[4], part), 71), part),
    }


def dft_table(first_sample, sample_count):
    samples = first_sample + jnp.arange(sample_count, dtype=jnp.int32)
    bin_index = K0 + jnp.arange(NB, dtype=jnp.int32)
    residue = samples[:, None] * bin_index[None, :] % WIN
    angles = residue.astype(jnp.float32) * (2.0 * math.pi / WIN)
    return jnp.concatenate([jnp.cos(angles), -jnp.sin(angles)], axis=1).astype(jnp.bfloat16)

def prepare(raw_block, valid_lengths):
    positions = jnp.arange(WIN, dtype=jnp.int32)
    inside = positions[None, None, :] < valid_lengths[:, :, None]
    values = raw_block.astype(jnp.float32)
    kept = jnp.where(inside, values, 0.0)
    average = lax.optimization_barrier(jnp.sum(kept, axis=-1)) / valid_lengths.astype(jnp.float32)
    taper = 0.5 - 0.5 * jnp.cos(positions.astype(jnp.float32) * (2.0 * math.pi / WIN))
    return jnp.where(inside, (values - average[:, :, None]) * taper[None, None, :], 0.0).astype(jnp.bfloat16)

def whiten(spectra):
    row_count = spectra.shape[0]
    grouped = spectra.reshape(row_count, 2, NB // SUB, SUB)
    power = lax.optimization_barrier(jnp.sum(grouped * grouped, axis=(1, 3))) / SUB
    factor = lax.rsqrt(power + 1e-06)
    return (grouped * factor[:, None, :, None]).reshape(row_count, 2, NB).astype(jnp.bfloat16)

def reference(raw, lengths, quality, assignment):
    shaped = prepare(raw, lengths)
    spectra = jnp.dot(shaped.reshape(CH * W, WIN), dft_table(0, WIN), preferred_element_type=jnp.float32)
    whitened = whiten(spectra).reshape(CH, W, 2, NB)
    whitened = whitened * quality.astype(jnp.bfloat16)[:, None, None, None]
    ordered = jnp.zeros_like(whitened).at[assignment].set(whitened)
    turned = jnp.stack([-ordered[:, :, 1], ordered[:, :, 0]], axis=2)
    left_all = ordered.transpose(3, 0, 2, 1).reshape(NB, CH, 2 * W).astype(jnp.float32)
    right_plain = ordered.transpose(3, 2, 1, 0).reshape(NB, 2 * W, CH).astype(jnp.float32)
    right_turned = turned.transpose(3, 2, 1, 0).reshape(NB, 2 * W, CH).astype(jnp.float32)
    left_blocks = left_all.reshape(NB, CH // CH_BLK, CH_BLK, 2 * W).transpose(1, 0, 2, 3)

    def one_block(left):
        real_part = jnp.einsum('bik,bkj->bij', left, right_plain, precision=lax.Precision.HIGHEST)
        imag_part = jnp.einsum('bik,bkj->bij', left, right_turned, precision=lax.Precision.HIGHEST)
        return (jnp.stack([real_part, imag_part], axis=2) / W).astype(jnp.bfloat16)
    blocks = lax.map(one_block, left_blocks)
    return blocks.transpose(1, 0, 2, 3, 4).reshape(NB, CH, 2, CH)
```

```python
import math

import jax
import jax.numpy as jnp
import ml_dtypes
import numpy as np
from jax import lax
from jax.sharding import PartitionSpec as P

WIN = 12000
NB = 512
K0 = 6
SUB = 32
QUARTER = WIN // 4


def quarter_table():
    samples = np.arange(QUARTER, dtype=np.int64)
    bins = K0 + np.arange(NB, dtype=np.int64)
    residue = samples[:, None] * bins[None, :] % WIN
    angles = residue.astype(np.float32) * np.float32(2.0 * math.pi / WIN)
    real = np.cos(angles).astype(ml_dtypes.bfloat16)
    imag = (-np.sin(angles)).astype(ml_dtypes.bfloat16)
    return real, imag


def turns():
    power = (np.arange(4)[:, None] * (K0 + np.arange(NB))[None, :]) % 4
    real = np.array([1.0, 0.0, -1.0, 0.0], np.float32)[power]
    imag = np.array([0.0, -1.0, 0.0, 1.0], np.float32)[power]
    return real, imag


def prepare(raw_block, valid_lengths):
    positions = jnp.arange(WIN, dtype=jnp.int32)
    inside = positions[None, None, :] < valid_lengths[:, :, None]
    values = raw_block.astype(jnp.float32)
    kept = jnp.where(inside, values, 0.0)
    average = jnp.sum(kept, axis=-1) / valid_lengths.astype(jnp.float32)
    taper = 0.5 - 0.5 * jnp.cos(positions.astype(jnp.float32) * (2.0 * math.pi / WIN))
    return jnp.where(inside, (values - average[:, :, None]) * taper[None, None, :], 0.0).astype(
        jnp.bfloat16
    )


def whiten(spectra):
    row_count = spectra.shape[0]
    grouped = spectra.reshape(row_count, 2, NB // SUB, SUB)
    power = jnp.sum(grouped * grouped, axis=(1, 3)) / SUB
    factor = lax.rsqrt(power + 1e-06)
    return (grouped * factor[:, None, :, None]).reshape(row_count, 2, NB).astype(jnp.bfloat16)


def spectra_of(shaped_rows):
    row_count = shaped_rows.shape[0]
    real_table, imag_table = quarter_table()
    table = jnp.asarray(np.concatenate([real_table, imag_table], axis=1))
    quarters = jnp.concatenate(
        [lax.slice_in_dim(shaped_rows, q * QUARTER, (q + 1) * QUARTER, axis=1) for q in range(4)], axis=0
    )
    parts = jnp.dot(quarters, table, preferred_element_type=jnp.float32).reshape(4, row_count, 2, NB)
    turn_real, turn_imag = (jnp.asarray(t)[:, None, :] for t in turns())
    real = jnp.sum(parts[:, :, 0] * turn_real - parts[:, :, 1] * turn_imag, axis=0)
    imag = jnp.sum(parts[:, :, 1] * turn_real + parts[:, :, 0] * turn_imag, axis=0)
    return whiten(jnp.concatenate([real, imag], axis=1))


def plain_body(raw, lengths, quality, assignment):
    my_index = lax.axis_index("chan")
    block_rows, window_count, sample_count = raw.shape
    total_channels = assignment.shape[0]
    my_quality = lax.dynamic_slice_in_dim(quality, my_index * block_rows, block_rows)
    shaped = prepare(raw, lengths)
    whitened = spectra_of(shaped.reshape(block_rows * window_count, sample_count)).reshape(
        block_rows, window_count, 2, NB
    )
    whitened = whitened * my_quality.astype(jnp.bfloat16)[:, None, None, None]
    panel = lax.all_to_all(whitened, "freq", split_axis=3, concat_axis=1, tiled=True)
    all_windows = panel.shape[1]
    gathered = lax.all_gather(panel, "chan", axis=0, tiled=True)
    positions = jnp.arange(total_channels, dtype=jnp.int32)
    place = (assignment[:, None] == positions[None, :]).astype(jnp.bfloat16)
    my_positions = my_index * block_rows + jnp.arange(block_rows, dtype=jnp.int32)
    my_place = (assignment[:, None] == my_positions[None, :]).astype(jnp.bfloat16)
    bins_here = gathered.shape[3]
    right = jnp.einsum("cwpb,cj->bpwj", gathered, place, preferred_element_type=jnp.float32)
    right = right.astype(jnp.bfloat16).reshape(bins_here, 2 * all_windows, total_channels)
    left = jnp.einsum("cwpb,ci->bipw", gathered, my_place, preferred_element_type=jnp.float32)
    left = left.astype(jnp.bfloat16)
    both = jnp.stack(
        [left, jnp.stack([left[:, :, 1], -left[:, :, 0]], axis=2)], axis=2
    ).reshape(bins_here, 2 * block_rows, 2 * all_windows)
    cross = jnp.einsum("bik,bkj->bij", both, right, preferred_element_type=jnp.float32)
    return (cross / all_windows).astype(jnp.bfloat16).reshape(bins_here, block_rows, 2, total_channels)


def solution(mesh):
    return jax.shard_map(
        plain_body,
        mesh=mesh,
        in_specs=(
            P(("groups", "chan"), "freq", None),
            P(("groups", "chan"), "freq"),
            P("groups"),
            P("groups"),
        ),
        out_specs=P("freq", ("groups", "chan"), None, None),
        check_vma=False,
    )
```

```python
import math

import jax
import jax.numpy as jnp
import ml_dtypes
import numpy as np
from jax import lax
from jax.experimental import pallas as pl
from jax.experimental.pallas import tpu as pltpu
from jax.sharding import PartitionSpec as P

WIN = 12000
NB = 512
K0 = 6
SUB = 32
QUARTER = WIN // 4


def quarter_table():
    samples = np.arange(QUARTER, dtype=np.int64)
    bins = K0 + np.arange(NB, dtype=np.int64)
    residue = samples[:, None] * bins[None, :] % WIN
    angles = residue.astype(np.float32) * np.float32(2.0 * math.pi / WIN)
    real = np.cos(angles).astype(ml_dtypes.bfloat16)
    imag = (-np.sin(angles)).astype(ml_dtypes.bfloat16)
    return real, imag


def turns():
    power = (np.arange(4)[:, None] * (K0 + np.arange(NB))[None, :]) % 4
    real = np.array([1.0, 0.0, -1.0, 0.0], np.float32)[power]
    imag = np.array([0.0, -1.0, 0.0, 1.0], np.float32)[power]
    return real, imag


def prepare(raw_block, valid_lengths):
    positions = jnp.arange(WIN, dtype=jnp.int32)
    inside = positions[None, None, :] < valid_lengths[:, :, None]
    values = raw_block.astype(jnp.float32)
    kept = jnp.where(inside, values, 0.0)
    average = jnp.sum(kept, axis=-1) / valid_lengths.astype(jnp.float32)
    taper = 0.5 - 0.5 * jnp.cos(positions.astype(jnp.float32) * (2.0 * math.pi / WIN))
    return jnp.where(inside, (values - average[:, :, None]) * taper[None, None, :], 0.0).astype(
        jnp.bfloat16
    )


def whiten(spectra):
    row_count = spectra.shape[0]
    grouped = spectra.reshape(row_count, 2, NB // SUB, SUB)
    power = jnp.sum(grouped * grouped, axis=(1, 3)) / SUB
    factor = lax.rsqrt(power + 1e-06)
    return (grouped * factor[:, None, :, None]).reshape(row_count, 2, NB).astype(jnp.bfloat16)


def spectra_of(shaped_rows):
    row_count = shaped_rows.shape[0]
    real_table, imag_table = quarter_table()
    table = jnp.asarray(np.concatenate([real_table, imag_table], axis=1))
    quarters = jnp.concatenate(
        [lax.slice_in_dim(shaped_rows, q * QUARTER, (q + 1) * QUARTER, axis=1) for q in range(4)], axis=0
    )
    parts = jnp.dot(quarters, table, preferred_element_type=jnp.float32).reshape(4, row_count, 2, NB)
    turn_real, turn_imag = (jnp.asarray(t)[:, None, :] for t in turns())
    real = jnp.sum(parts[:, :, 0] * turn_real - parts[:, :, 1] * turn_imag, axis=0)
    imag = jnp.sum(parts[:, :, 1] * turn_real + parts[:, :, 0] * turn_imag, axis=0)
    return whiten(jnp.concatenate([real, imag], axis=1))


def plain_body(raw, lengths, quality, assignment):
    my_index = lax.axis_index("chan")
    block_rows, window_count, sample_count = raw.shape
    total_channels = assignment.shape[0]
    my_quality = lax.dynamic_slice_in_dim(quality, my_index * block_rows, block_rows)
    shaped = prepare(raw, lengths)
    whitened = spectra_of(shaped.reshape(block_rows * window_count, sample_count)).reshape(
        block_rows, window_count, 2, NB
    )
    whitened = whitened * my_quality.astype(jnp.bfloat16)[:, None, None, None]
    panel = lax.all_to_all(whitened, "freq", split_axis=3, concat_axis=1, tiled=True)
    all_windows = panel.shape[1]
    gathered = lax.all_gather(panel, "chan", axis=0, tiled=True)
    positions = jnp.arange(total_channels, dtype=jnp.int32)
    place = (assignment[:, None] == positions[None, :]).astype(jnp.bfloat16)
    my_positions = my_index * block_rows + jnp.arange(block_rows, dtype=jnp.int32)
    my_place = (assignment[:, None] == my_positions[None, :]).astype(jnp.bfloat16)
    bins_here = gathered.shape[3]
    right = jnp.einsum("cwpb,cj->bpwj", gathered, place, preferred_element_type=jnp.float32)
    right = right.astype(jnp.bfloat16).reshape(bins_here, 2 * all_windows, total_channels)
    left = jnp.einsum("cwpb,ci->bipw", gathered, my_place, preferred_element_type=jnp.float32)
    left = left.astype(jnp.bfloat16)
    both = jnp.stack(
        [left, jnp.stack([left[:, :, 1], -left[:, :, 0]], axis=2)], axis=2
    ).reshape(bins_here, 2 * block_rows, 2 * all_windows)
    cross = jnp.einsum("bik,bkj->bij", both, right, preferred_element_type=jnp.float32)
    return (cross / all_windows).astype(jnp.bfloat16).reshape(bins_here, block_rows, 2, total_channels)


CHUNK = 128
DEPTH = 3072
MESH = pl.DeviceIdType.MESH


def spectra_kernel(raw_ref, length_ref, taper_ref, order_ref, turn_ref, group_ref, table_ref, out_ref, rows):
    row_count = raw_ref.shape[0]

    @pl.when(pl.program_id(0) == 0)
    def _():
        rows[:, QUARTER // 128 * 128 :] = jnp.zeros(
            (4 * row_count, DEPTH - QUARTER // 128 * 128), jnp.bfloat16
        )
        taper = taper_ref[...]

        def prepare_rows(step, carry):
            first = pl.multiple_of(step * 16, 16)
            values = raw_ref[pl.ds(first, 16), :].astype(jnp.float32)
            valid = length_ref[pl.ds(first, 16), :]
            inside = lax.broadcasted_iota(jnp.int32, (16, WIN), 1) < valid
            kept = jnp.where(inside, values, 0.0)
            average = jnp.sum(kept, axis=1, keepdims=True) / valid.astype(jnp.float32)
            shaped = jnp.where(inside, (values - average) * taper, 0.0)
            for q in range(4):
                rows[pl.ds(pl.multiple_of(q * row_count + first, 16), 16), :QUARTER] = shaped[
                    :, q * QUARTER : (q + 1) * QUARTER
                ].astype(jnp.bfloat16)
            return carry

        lax.fori_loop(0, row_count // 16, prepare_rows, 0)

    parts = jnp.dot(rows[...], table_ref[0], preferred_element_type=jnp.float32)
    real = jnp.zeros((row_count, CHUNK), jnp.float32)
    imag = jnp.zeros((row_count, CHUNK), jnp.float32)
    for q in range(4):
        a = parts[q * row_count : (q + 1) * row_count, :CHUNK]
        b = parts[q * row_count : (q + 1) * row_count, CHUNK:]
        turn_real, turn_imag = turn_ref[q : q + 1, :], turn_ref[4 + q : 5 + q, :]
        real += a * turn_real - b * turn_imag
        imag += b * turn_real + a * turn_imag
    power = jnp.dot(
        real * real + imag * imag,
        group_ref[...],
        preferred_element_type=jnp.float32,
        precision=lax.Precision.HIGHEST,
    )
    factor = lax.rsqrt(power / SUB + 1e-06)
    for part, value in enumerate((real, imag)):
        out_ref[0, part * row_count : (part + 1) * row_count, :] = jnp.dot(
            order_ref[...], (value * factor).astype(jnp.bfloat16), preferred_element_type=jnp.float32
        ).astype(jnp.bfloat16)


def gather_kernel(own_ref, out_ref, local_sem, arrive, up_sem, down_sem, side_sem, core_sem):
    chunks = own_ref.shape[0]
    levels = out_ref.shape[0] // 4
    me = lax.axis_index("chan")
    core = lax.rem(me, 2)
    side = lax.rem(me // 2, 2)
    level = me // 4
    up, down = me + 4, me - 4
    beside = level * 4 + (1 - side) * 2 + core
    partner = level * 4 + side * 2 + (1 - core)
    has_up, has_down = level < levels - 1, level > 0

    barrier = pltpu.get_barrier_semaphore()

    def greet(target):
        pl.semaphore_signal(barrier, inc=1, device_id={"chan": target}, device_id_type=MESH)

    greet(beside)
    greet(partner)
    pl.when(has_up)(lambda: greet(up))
    pl.when(has_down)(lambda: greet(down))
    pl.semaphore_wait(barrier, 2 + has_up.astype(jnp.int32) + has_down.astype(jnp.int32))

    keep = pltpu.make_async_copy(own_ref, out_ref.at[me], local_sem)
    keep.start()

    def copy(kind, target, origin, chunk, mine=False):
        slot = {"up": origin // 4, "down": origin // 4, "side": origin // 4, "core": origin // 2}[kind]
        sems = {"up": up_sem, "down": down_sem, "side": side_sem, "core": core_sem}[kind]
        return pltpu.make_async_remote_copy(
            src_ref=own_ref.at[chunk] if mine else out_ref.at[origin, chunk],
            dst_ref=out_ref.at[origin, chunk],
            send_sem=sems.at[slot, chunk],
            recv_sem=arrive.at[origin, chunk],
            device_id={"chan": target},
            device_id_type=MESH,
        )

    def landed(origin, chunk):
        copy("core", partner, origin, chunk).wait_recv()

    def send_own(chunk, carry):
        copy("side", beside, me, chunk, True).start()
        pl.when(has_up)(lambda: copy("up", up, me, chunk, True).start())
        pl.when(has_down)(lambda: copy("down", down, me, chunk, True).start())
        copy("core", partner, me, chunk, True).start()
        return carry

    lax.fori_loop(0, chunks, send_own, 0)

    def from_side(distance, chunk):
        def pass_on(origin):
            landed(origin, chunk)
            copy("core", partner, origin, chunk).start()

        if distance == 0:
            pass_on(beside)
        else:
            pl.when(level >= distance)(lambda: pass_on(beside - 4 * distance))
            pl.when(level + distance < levels)(lambda: pass_on(beside + 4 * distance))

    for distance in range(1, levels + 1):

        def step(chunk, carry, distance=distance):
            def below():
                origin = me - 4 * distance
                landed(origin, chunk)
                copy("side", beside, origin, chunk).start()
                pl.when(has_up)(lambda: copy("up", up, origin, chunk).start())
                copy("core", partner, origin, chunk).start()

            def above():
                origin = me + 4 * distance
                landed(origin, chunk)
                copy("side", beside, origin, chunk).start()
                pl.when(has_down)(lambda: copy("down", down, origin, chunk).start())
                copy("core", partner, origin, chunk).start()

            if distance < levels:
                pl.when(level >= distance)(below)
                pl.when(level + distance < levels)(above)
            from_side(distance - 1, chunk)
            return carry

        lax.fori_loop(0, chunks, step, 0)

    def finish(chunk, carry):
        for z in range(levels):
            for y in range(2):
                landed(z * 4 + y * 2 + (1 - core), chunk)
        for z in range(levels):
            line = z * 4 + side * 2 + core
            copy("side", beside, line, chunk).wait_send()
            copy("core", partner, line, chunk).wait_send()
            copy("core", partner, z * 4 + (1 - side) * 2 + core, chunk).wait_send()
            pl.when(jnp.logical_and(has_up, z <= level))(
                lambda line=line: copy("up", up, line, chunk).wait_send()
            )
            pl.when(jnp.logical_and(has_down, z >= level))(
                lambda line=line: copy("down", down, line, chunk).wait_send()
            )
        return carry

    lax.fori_loop(0, chunks, finish, 0)
    keep.wait()


def cross_kernel(panel_ref, place_ref, select_ref, out_ref, right, *, window_count):
    depth = 2 * window_count
    devices = panel_ref.shape[0]
    for pair in range(window_count):
        block = panel_ref[:, 0, pair * 16 : (pair + 1) * 16, :].reshape(devices * 16, CHUNK)
        turned = lax.dot_general(
            block, place_ref[...], (((0,), (0,)), ((), ())), preferred_element_type=jnp.float32
        )
        for half in range(2):
            right[pl.ds(pair * 2 + half, CHUNK, stride=depth), :] = turned[:, half * 128 : (half + 1) * 128]

    owner = lax.broadcasted_iota(jnp.int32, (8 * depth, 128), 0) // depth
    column = lax.broadcasted_iota(jnp.int32, (8 * depth, 128), 1) // 16
    mask = owner == column

    def one_group(group, carry):
        plain = right[pl.ds(pl.multiple_of(group * 8 * depth, 8 * depth), 8 * depth), :]
        split = plain.reshape(8, 2, window_count, 128)
        swapped = jnp.concatenate([split[:, 1:], -split[:, :1]], axis=1).reshape(8 * depth, 128)
        plain = plain.astype(jnp.bfloat16)
        both = jnp.concatenate([plain, swapped.astype(jnp.bfloat16)], axis=1)
        left = jnp.dot(both, select_ref[...], preferred_element_type=jnp.float32)
        left = jnp.where(mask, left, 0.0).astype(jnp.bfloat16)
        result = lax.dot_general(left, plain, (((0,), (0,)), ((), ())), preferred_element_type=jnp.float32)
        out_ref[pl.ds(pl.multiple_of(group * 128, 128), 128), :] = (result * (1.0 / window_count)).astype(
            jnp.bfloat16
        )
        return carry

    lax.fori_loop(0, CHUNK // 8, one_group, 0)


def kernel_body(raw, lengths, quality, assignment):
    me = lax.axis_index("chan")
    block_rows, window_count, _ = raw.shape
    row_count = block_rows * window_count
    total_channels = assignment.shape[0]
    devices = total_channels // block_rows
    chunks = NB // CHUNK
    real_table, imag_table = quarter_table()
    table = np.zeros((chunks, DEPTH, 2 * CHUNK), ml_dtypes.bfloat16)
    for chunk in range(chunks):
        table[chunk, :QUARTER, :CHUNK] = real_table[:, chunk * CHUNK : (chunk + 1) * CHUNK]
        table[chunk, :QUARTER, CHUNK:] = imag_table[:, chunk * CHUNK : (chunk + 1) * CHUNK]
    turn = np.concatenate(turns(), axis=0)[:, :CHUNK]
    positions = np.arange(WIN, dtype=np.float32)
    taper = (0.5 - 0.5 * np.cos(positions * np.float32(2.0 * math.pi / WIN))).astype(np.float32)[None, :]
    lanes = np.arange(CHUNK)
    group = (lanes[:, None] // SUB == lanes[None, :] // SUB).astype(np.float32)
    flat = np.arange(row_count)
    shuffle = (
        (flat[:, None] // block_rows == flat[None, :] % window_count)
        & (flat[:, None] % block_rows == flat[None, :] // window_count)
    ).astype(np.float32)
    my_quality = lax.dynamic_slice_in_dim(quality, me * block_rows, block_rows).astype(jnp.float32)
    order = (jnp.asarray(shuffle) * jnp.repeat(my_quality, window_count)[None, :]).astype(jnp.bfloat16)

    def whole(shape):
        return pl.BlockSpec(shape, lambda j: (0,) * len(shape))

    own = pl.pallas_call(
        spectra_kernel,
        grid=(chunks,),
        in_specs=[
            whole((row_count, WIN)),
            whole((row_count, 1)),
            whole((1, WIN)),
            whole((row_count, row_count)),
            whole((8, CHUNK)),
            whole((CHUNK, CHUNK)),
            pl.BlockSpec((1, DEPTH, 2 * CHUNK), lambda j: (j, 0, 0)),
        ],
        out_specs=pl.BlockSpec((1, 2 * row_count, CHUNK), lambda j: (j, 0, 0)),
        out_shape=jax.ShapeDtypeStruct((chunks, 2 * row_count, CHUNK), jnp.bfloat16),
        scratch_shapes=[pltpu.VMEM((4 * row_count, DEPTH), jnp.bfloat16)],
        compiler_params=pltpu.CompilerParams(vmem_limit_bytes=48 * 2**20),
    )(
        raw.reshape(row_count, WIN),
        lengths.reshape(row_count, 1),
        jnp.asarray(taper),
        order,
        jnp.asarray(turn),
        jnp.asarray(group),
        jnp.asarray(table),
    )

    panel = pl.pallas_call(
        gather_kernel,
        in_specs=[pl.BlockSpec(memory_space=pl.ANY)],
        out_specs=pl.BlockSpec(memory_space=pl.ANY),
        out_shape=jax.ShapeDtypeStruct((devices, chunks, 2 * row_count, CHUNK), jnp.bfloat16),
        scratch_shapes=[
            pltpu.SemaphoreType.DMA,
            pltpu.SemaphoreType.DMA((devices, chunks)),
            pltpu.SemaphoreType.DMA((devices // 4, chunks)),
            pltpu.SemaphoreType.DMA((devices // 4, chunks)),
            pltpu.SemaphoreType.DMA((devices // 4, chunks)),
            pltpu.SemaphoreType.DMA((devices // 2, chunks)),
        ],
        compiler_params=pltpu.CompilerParams(collective_id=0, has_side_effects=True),
    )(own)

    spot = jnp.repeat(assignment.reshape(devices, 1, block_rows), 2, axis=1).reshape(-1)
    half = (np.arange(2 * total_channels) // block_rows) % 2
    columns = np.arange(2 * total_channels)
    place = jnp.logical_and(
        spot[:, None] == jnp.asarray(columns % total_channels)[None, :],
        jnp.asarray(half[:, None] == columns[None, :] // total_channels),
    ).astype(jnp.bfloat16)
    column = np.arange(128)
    source = np.arange(2 * total_channels)
    select = jnp.logical_and(
        jnp.asarray(source % total_channels)[:, None]
        == me * block_rows + jnp.asarray(column // 2 % block_rows)[None, :],
        jnp.asarray((source // total_channels)[:, None] == (column % 2)[None, :]),
    ).astype(jnp.bfloat16)
    cross = pl.pallas_call(
        lambda *refs: cross_kernel(*refs, window_count=window_count),
        grid=(chunks,),
        in_specs=[
            pl.BlockSpec((devices, 1, 2 * row_count, CHUNK), lambda j: (0, j, 0, 0)),
            whole((2 * total_channels, 2 * total_channels)),
            whole((2 * total_channels, 128)),
        ],
        out_specs=pl.BlockSpec((CHUNK * 2 * block_rows, total_channels), lambda j: (j, 0)),
        out_shape=jax.ShapeDtypeStruct((NB * 2 * block_rows, total_channels), jnp.bfloat16),
        scratch_shapes=[pltpu.VMEM((CHUNK * 2 * window_count, total_channels), jnp.float32)],
        compiler_params=pltpu.CompilerParams(vmem_limit_bytes=48 * 2**20),
    )(panel, place, select)
    return cross.reshape(NB, block_rows, 2, total_channels)


def solution(mesh):
    ours = mesh.shape["freq"] == 1 and mesh.shape["chan"] == 16
    return jax.shard_map(
        kernel_body if ours else plain_body,
        mesh=mesh,
        in_specs=(
            P(("groups", "chan"), "freq", None),
            P(("groups", "chan"), "freq"),
            P("groups"),
            P("groups"),
        ),
        out_specs=P("freq", ("groups", "chan"), None, None),
        check_vma=False,
    )
```

```python
import functools
import math

import jax
import jax.numpy as jnp
import ml_dtypes
import numpy as np
from jax import lax
from jax.experimental import pallas as pl
from jax.experimental.pallas import tpu as pltpu
from jax.sharding import PartitionSpec as P

WIN = 12000
NB = 512
K0 = 6
SUB = 32
QUARTER = WIN // 4


def quarter_table():
    samples = np.arange(QUARTER, dtype=np.int64)
    bins = K0 + np.arange(NB, dtype=np.int64)
    residue = samples[:, None] * bins[None, :] % WIN
    angles = residue.astype(np.float32) * np.float32(2.0 * math.pi / WIN)
    real = np.cos(angles).astype(ml_dtypes.bfloat16)
    imag = (-np.sin(angles)).astype(ml_dtypes.bfloat16)
    return real, imag


def turns():
    power = (np.arange(4)[:, None] * (K0 + np.arange(NB))[None, :]) % 4
    real = np.array([1.0, 0.0, -1.0, 0.0], np.float32)[power]
    imag = np.array([0.0, -1.0, 0.0, 1.0], np.float32)[power]
    return real, imag


def prepare(raw_block, valid_lengths):
    positions = jnp.arange(WIN, dtype=jnp.int32)
    inside = positions[None, None, :] < valid_lengths[:, :, None]
    values = raw_block.astype(jnp.float32)
    kept = jnp.where(inside, values, 0.0)
    average = jnp.sum(kept, axis=-1) / valid_lengths.astype(jnp.float32)
    taper = 0.5 - 0.5 * jnp.cos(positions.astype(jnp.float32) * (2.0 * math.pi / WIN))
    return jnp.where(inside, (values - average[:, :, None]) * taper[None, None, :], 0.0).astype(
        jnp.bfloat16
    )


def whiten(spectra):
    row_count = spectra.shape[0]
    grouped = spectra.reshape(row_count, 2, NB // SUB, SUB)
    power = jnp.sum(grouped * grouped, axis=(1, 3)) / SUB
    factor = lax.rsqrt(power + 1e-06)
    return (grouped * factor[:, None, :, None]).reshape(row_count, 2, NB).astype(jnp.bfloat16)


def spectra_of(shaped_rows):
    row_count = shaped_rows.shape[0]
    real_table, imag_table = quarter_table()
    table = jnp.asarray(np.concatenate([real_table, imag_table], axis=1))
    quarters = jnp.concatenate(
        [lax.slice_in_dim(shaped_rows, q * QUARTER, (q + 1) * QUARTER, axis=1) for q in range(4)], axis=0
    )
    parts = jnp.dot(quarters, table, preferred_element_type=jnp.float32).reshape(4, row_count, 2, NB)
    turn_real, turn_imag = (jnp.asarray(t)[:, None, :] for t in turns())
    real = jnp.sum(parts[:, :, 0] * turn_real - parts[:, :, 1] * turn_imag, axis=0)
    imag = jnp.sum(parts[:, :, 1] * turn_real + parts[:, :, 0] * turn_imag, axis=0)
    return whiten(jnp.concatenate([real, imag], axis=1))


def plain_body(raw, lengths, quality, assignment):
    my_index = lax.axis_index("chan")
    block_rows, window_count, sample_count = raw.shape
    total_channels = assignment.shape[0]
    my_quality = lax.dynamic_slice_in_dim(quality, my_index * block_rows, block_rows)
    shaped = prepare(raw, lengths)
    whitened = spectra_of(shaped.reshape(block_rows * window_count, sample_count)).reshape(
        block_rows, window_count, 2, NB
    )
    whitened = whitened * my_quality.astype(jnp.bfloat16)[:, None, None, None]
    panel = lax.all_to_all(whitened, "freq", split_axis=3, concat_axis=1, tiled=True)
    all_windows = panel.shape[1]
    gathered = lax.all_gather(panel, "chan", axis=0, tiled=True)
    positions = jnp.arange(total_channels, dtype=jnp.int32)
    place = (assignment[:, None] == positions[None, :]).astype(jnp.bfloat16)
    my_positions = my_index * block_rows + jnp.arange(block_rows, dtype=jnp.int32)
    my_place = (assignment[:, None] == my_positions[None, :]).astype(jnp.bfloat16)
    bins_here = gathered.shape[3]
    right = jnp.einsum("cwpb,cj->bpwj", gathered, place, preferred_element_type=jnp.float32)
    right = right.astype(jnp.bfloat16).reshape(bins_here, 2 * all_windows, total_channels)
    left = jnp.einsum("cwpb,ci->bipw", gathered, my_place, preferred_element_type=jnp.float32)
    left = left.astype(jnp.bfloat16)
    both = jnp.stack(
        [left, jnp.stack([left[:, :, 1], -left[:, :, 0]], axis=2)], axis=2
    ).reshape(bins_here, 2 * block_rows, 2 * all_windows)
    cross = jnp.einsum("bik,bkj->bij", both, right, preferred_element_type=jnp.float32)
    return (cross / all_windows).astype(jnp.bfloat16).reshape(bins_here, block_rows, 2, total_channels)


CHUNK = 128
DEPTH = 3072
MESH = pl.DeviceIdType.MESH


def spectra_kernel(raw_ref, length_ref, taper_ref, order_ref, turn_ref, group_ref, table_ref, out_ref, rows):
    row_count = raw_ref.shape[0]

    @pl.when(pl.program_id(0) == 0)
    def _():
        rows[:, QUARTER // 128 * 128 :] = jnp.zeros(
            (4 * row_count, DEPTH - QUARTER // 128 * 128), jnp.bfloat16
        )
        taper = taper_ref[...]

        def prepare_rows(step, carry):
            first = pl.multiple_of(step * 16, 16)
            values = raw_ref[pl.ds(first, 16), :].astype(jnp.float32)
            valid = length_ref[pl.ds(first, 16), :]
            inside = lax.broadcasted_iota(jnp.int32, (16, WIN), 1) < valid
            kept = jnp.where(inside, values, 0.0)
            average = jnp.sum(kept, axis=1, keepdims=True) / valid.astype(jnp.float32)
            shaped = jnp.where(inside, (values - average) * taper, 0.0)
            for q in range(4):
                rows[pl.ds(pl.multiple_of(q * row_count + first, 16), 16), :QUARTER] = shaped[
                    :, q * QUARTER : (q + 1) * QUARTER
                ].astype(jnp.bfloat16)
            return carry

        lax.fori_loop(0, row_count // 16, prepare_rows, 0)

    parts = jnp.dot(rows[...], table_ref[0], preferred_element_type=jnp.float32)
    real = jnp.zeros((row_count, CHUNK), jnp.float32)
    imag = jnp.zeros((row_count, CHUNK), jnp.float32)
    for q in range(4):
        a = parts[q * row_count : (q + 1) * row_count, :CHUNK]
        b = parts[q * row_count : (q + 1) * row_count, CHUNK:]
        turn_real, turn_imag = turn_ref[q : q + 1, :], turn_ref[4 + q : 5 + q, :]
        real += a * turn_real - b * turn_imag
        imag += b * turn_real + a * turn_imag
    power = jnp.dot(
        real * real + imag * imag,
        group_ref[...],
        preferred_element_type=jnp.float32,
        precision=lax.Precision.HIGHEST,
    )
    factor = lax.rsqrt(power / SUB + 1e-06)
    for part, value in enumerate((real, imag)):
        out_ref[0, part * row_count : (part + 1) * row_count, :] = jnp.dot(
            order_ref[...], (value * factor).astype(jnp.bfloat16), preferred_element_type=jnp.float32
        ).astype(jnp.bfloat16)


def cross_kernel(
    own_ref,
    place_ref,
    select_ref,
    out_ref,
    panel,
    right,
    local_sem,
    arrive,
    up_sem,
    down_sem,
    side_sem,
    core_sem,
    *,
    window_count,
):
    chunks = own_ref.shape[0]
    levels = panel.shape[0] // 4
    me = lax.axis_index("chan")
    core = lax.rem(me, 2)
    side = lax.rem(me // 2, 2)
    level = me // 4
    up, down = me + 4, me - 4
    beside = level * 4 + (1 - side) * 2 + core
    partner = level * 4 + side * 2 + (1 - core)
    has_up, has_down = level < levels - 1, level > 0

    barrier = pltpu.get_barrier_semaphore()

    def greet(target):
        pl.semaphore_signal(barrier, inc=1, device_id={"chan": target}, device_id_type=MESH)

    greet(beside)
    greet(partner)
    pl.when(has_up)(lambda: greet(up))
    pl.when(has_down)(lambda: greet(down))
    pl.semaphore_wait(barrier, 2 + has_up.astype(jnp.int32) + has_down.astype(jnp.int32))

    keep = pltpu.make_async_copy(own_ref, panel.at[me], local_sem)
    keep.start()

    def copy(kind, target, origin, chunk, mine=False):
        slot = {"up": origin // 4, "down": origin // 4, "side": origin // 4, "core": origin // 2}[kind]
        sems = {"up": up_sem, "down": down_sem, "side": side_sem, "core": core_sem}[kind]
        return pltpu.make_async_remote_copy(
            src_ref=own_ref.at[chunk] if mine else panel.at[origin, chunk],
            dst_ref=panel.at[origin, chunk],
            send_sem=sems.at[slot, chunk],
            recv_sem=arrive.at[origin, chunk],
            device_id={"chan": target},
            device_id_type=MESH,
        )

    def landed(origin, chunk):
        copy("core", partner, origin, chunk).wait_recv()

    def send_own(chunk, carry):
        copy("side", beside, me, chunk, True).start()
        pl.when(has_up)(lambda: copy("up", up, me, chunk, True).start())
        pl.when(has_down)(lambda: copy("down", down, me, chunk, True).start())
        copy("core", partner, me, chunk, True).start()
        return carry

    lax.fori_loop(0, chunks, send_own, 0)

    def from_side(distance, chunk):
        def pass_on(origin):
            landed(origin, chunk)
            copy("core", partner, origin, chunk).start()

        if distance == 0:
            pass_on(beside)
        else:
            pl.when(level >= distance)(lambda: pass_on(beside - 4 * distance))
            pl.when(level + distance < levels)(lambda: pass_on(beside + 4 * distance))

    def relay(distance, chunk):
        def below():
            origin = me - 4 * distance
            landed(origin, chunk)
            copy("side", beside, origin, chunk).start()
            pl.when(has_up)(lambda: copy("up", up, origin, chunk).start())
            copy("core", partner, origin, chunk).start()

        def above():
            origin = me + 4 * distance
            landed(origin, chunk)
            copy("side", beside, origin, chunk).start()
            pl.when(has_down)(lambda: copy("down", down, origin, chunk).start())
            copy("core", partner, origin, chunk).start()

        if distance < levels:
            pl.when(level >= distance)(below)
            pl.when(level + distance < levels)(above)
        from_side(distance - 1, chunk)

    depth = 2 * window_count
    devices = panel.shape[0]
    owner = lax.broadcasted_iota(jnp.int32, (8 * depth, 128), 0) // depth
    column = lax.broadcasted_iota(jnp.int32, (8 * depth, 128), 1) // 16
    mask = owner == column

    def arrange(chunk):
        for pair in range(window_count):
            block = panel[:, chunk, pair * 16 : (pair + 1) * 16, :].reshape(devices * 16, CHUNK)
            turned = lax.dot_general(
                block, place_ref[...], (((0,), (0,)), ((), ())), preferred_element_type=jnp.float32
            )
            for half in range(2):
                right[pl.ds(pair * 2 + half, CHUNK, stride=depth), :] = turned[:, half * 128 : (half + 1) * 128]

    def multiply(chunk, first, last):
        for group in range(first, last):
            plain = right[group * 8 * depth : (group + 1) * 8 * depth, :]
            split = plain.reshape(8, 2, window_count, 128)
            swapped = jnp.concatenate([split[:, 1:], -split[:, :1]], axis=1).reshape(8 * depth, 128)
            plain = plain.astype(jnp.bfloat16)
            both = jnp.concatenate([plain, swapped.astype(jnp.bfloat16)], axis=1)
            left = jnp.dot(both, select_ref[...], preferred_element_type=jnp.float32)
            left = jnp.where(mask, left, 0.0).astype(jnp.bfloat16)
            result = lax.dot_general(left, plain, (((0,), (0,)), ((), ())), preferred_element_type=jnp.float32)
            row = pl.multiple_of((chunk * (CHUNK // 8) + group) * 128, 128)
            out_ref[pl.ds(row, 128), :] = (result * (1.0 / window_count)).astype(jnp.bfloat16)

    groups = CHUNK // 8

    def advance(step, carry):
        for distance in range(1, levels + 1):
            pl.when(step < chunks)(lambda distance=distance: relay(distance, step))

            @pl.when(step > 0)
            def _(distance=distance):
                if distance == 1:
                    arrange(step - 1)
                else:
                    multiply(
                        step - 1,
                        groups * (distance - 2) // (levels - 1),
                        groups * (distance - 1) // (levels - 1),
                    )

        @pl.when(step < chunks)
        def _():
            for z in range(levels):
                for y in range(2):
                    landed(z * 4 + y * 2 + (1 - core), step)

        return carry

    keep.wait()
    lax.fori_loop(0, chunks + 1, advance, 0)

    def finish(chunk, carry):
        for z in range(levels):
            line = z * 4 + side * 2 + core
            copy("side", beside, line, chunk).wait_send()
            copy("core", partner, line, chunk).wait_send()
            copy("core", partner, z * 4 + (1 - side) * 2 + core, chunk).wait_send()
            pl.when(jnp.logical_and(has_up, z <= level))(
                lambda line=line: copy("up", up, line, chunk).wait_send()
            )
            pl.when(jnp.logical_and(has_down, z >= level))(
                lambda line=line: copy("down", down, line, chunk).wait_send()
            )
        return carry

    lax.fori_loop(0, chunks, finish, 0)


def kernel_body(raw, lengths, quality, assignment):
    me = lax.axis_index("chan")
    block_rows, window_count, _ = raw.shape
    row_count = block_rows * window_count
    total_channels = assignment.shape[0]
    devices = total_channels // block_rows
    chunks = NB // CHUNK
    real_table, imag_table = quarter_table()
    table = np.zeros((chunks, DEPTH, 2 * CHUNK), ml_dtypes.bfloat16)
    for chunk in range(chunks):
        table[chunk, :QUARTER, :CHUNK] = real_table[:, chunk * CHUNK : (chunk + 1) * CHUNK]
        table[chunk, :QUARTER, CHUNK:] = imag_table[:, chunk * CHUNK : (chunk + 1) * CHUNK]
    turn = np.concatenate(turns(), axis=0)[:, :CHUNK]
    positions = np.arange(WIN, dtype=np.float32)
    taper = (0.5 - 0.5 * np.cos(positions * np.float32(2.0 * math.pi / WIN))).astype(np.float32)[None, :]
    lanes = np.arange(CHUNK)
    group = (lanes[:, None] // SUB == lanes[None, :] // SUB).astype(np.float32)
    flat = np.arange(row_count)
    shuffle = (
        (flat[:, None] // block_rows == flat[None, :] % window_count)
        & (flat[:, None] % block_rows == flat[None, :] // window_count)
    ).astype(np.float32)
    my_quality = lax.dynamic_slice_in_dim(quality, me * block_rows, block_rows).astype(jnp.float32)
    order = (jnp.asarray(shuffle) * jnp.repeat(my_quality, window_count)[None, :]).astype(jnp.bfloat16)

    def whole(shape):
        return pl.BlockSpec(shape, lambda j: (0,) * len(shape))

    own = pl.pallas_call(
        spectra_kernel,
        grid=(chunks,),
        in_specs=[
            whole((row_count, WIN)),
            whole((row_count, 1)),
            whole((1, WIN)),
            whole((row_count, row_count)),
            whole((8, CHUNK)),
            whole((CHUNK, CHUNK)),
            pl.BlockSpec((1, DEPTH, 2 * CHUNK), lambda j: (j, 0, 0)),
        ],
        out_specs=pl.BlockSpec((1, 2 * row_count, CHUNK), lambda j: (j, 0, 0)),
        out_shape=jax.ShapeDtypeStruct((chunks, 2 * row_count, CHUNK), jnp.bfloat16),
        scratch_shapes=[pltpu.VMEM((4 * row_count, DEPTH), jnp.bfloat16)],
        compiler_params=pltpu.CompilerParams(vmem_limit_bytes=48 * 2**20),
    )(
        raw.reshape(row_count, WIN),
        lengths.reshape(row_count, 1),
        jnp.asarray(taper),
        order,
        jnp.asarray(turn),
        jnp.asarray(group),
        jnp.asarray(table),
    )

    spot = jnp.repeat(assignment.reshape(devices, 1, block_rows), 2, axis=1).reshape(-1)
    half = (np.arange(2 * total_channels) // block_rows) % 2
    columns = np.arange(2 * total_channels)
    place = jnp.logical_and(
        spot[:, None] == jnp.asarray(columns % total_channels)[None, :],
        jnp.asarray(half[:, None] == columns[None, :] // total_channels),
    ).astype(jnp.bfloat16)
    column = np.arange(128)
    source = np.arange(2 * total_channels)
    select = jnp.logical_and(
        jnp.asarray(source % total_channels)[:, None]
        == me * block_rows + jnp.asarray(column // 2 % block_rows)[None, :],
        jnp.asarray((source // total_channels)[:, None] == (column % 2)[None, :]),
    ).astype(jnp.bfloat16)
    vmem = pl.BlockSpec(memory_space=pltpu.VMEM)
    cross = pl.pallas_call(
        functools.partial(cross_kernel, window_count=window_count),
        in_specs=[vmem] * 3,
        out_specs=vmem,
        out_shape=jax.ShapeDtypeStruct((NB * 2 * block_rows, total_channels), jnp.bfloat16),
        scratch_shapes=[
            pltpu.VMEM((devices, chunks, 2 * row_count, CHUNK), jnp.bfloat16),
            pltpu.VMEM((CHUNK * 2 * window_count, total_channels), jnp.float32),
            pltpu.SemaphoreType.DMA,
            pltpu.SemaphoreType.DMA((devices, chunks)),
            pltpu.SemaphoreType.DMA((devices // 4, chunks)),
            pltpu.SemaphoreType.DMA((devices // 4, chunks)),
            pltpu.SemaphoreType.DMA((devices // 4, chunks)),
            pltpu.SemaphoreType.DMA((devices // 2, chunks)),
        ],
        compiler_params=pltpu.CompilerParams(
            collective_id=0, has_side_effects=True, vmem_limit_bytes=48 * 2**20
        ),
    )(own, place, select)
    return cross.reshape(NB, block_rows, 2, total_channels)


def solution(mesh):
    ours = mesh.shape["freq"] == 1 and mesh.shape["chan"] == 16
    return jax.shard_map(
        kernel_body if ours else plain_body,
        mesh=mesh,
        in_specs=(
            P(("groups", "chan"), "freq", None),
            P(("groups", "chan"), "freq"),
            P("groups"),
            P("groups"),
        ),
        out_specs=P("freq", ("groups", "chan"), None, None),
        check_vma=False,
    )
```

```python
import functools
import math

import jax
import jax.numpy as jnp
import ml_dtypes
import numpy as np
from jax import lax
from jax.experimental import pallas as pl
from jax.experimental.pallas import tpu as pltpu
from jax.sharding import PartitionSpec as P

WIN = 12000
NB = 512
K0 = 6
SUB = 32
QUARTER = WIN // 4


def quarter_table():
    samples = np.arange(QUARTER, dtype=np.int64)
    bins = K0 + np.arange(NB, dtype=np.int64)
    residue = samples[:, None] * bins[None, :] % WIN
    angles = residue.astype(np.float32) * np.float32(2.0 * math.pi / WIN)
    real = np.cos(angles).astype(ml_dtypes.bfloat16)
    imag = (-np.sin(angles)).astype(ml_dtypes.bfloat16)
    return real, imag


def turns():
    power = (np.arange(4)[:, None] * (K0 + np.arange(NB))[None, :]) % 4
    real = np.array([1.0, 0.0, -1.0, 0.0], np.float32)[power]
    imag = np.array([0.0, -1.0, 0.0, 1.0], np.float32)[power]
    return real, imag


def prepare(raw_block, valid_lengths):
    positions = jnp.arange(WIN, dtype=jnp.int32)
    inside = positions[None, None, :] < valid_lengths[:, :, None]
    values = raw_block.astype(jnp.float32)
    kept = jnp.where(inside, values, 0.0)
    average = jnp.sum(kept, axis=-1) / valid_lengths.astype(jnp.float32)
    taper = 0.5 - 0.5 * jnp.cos(positions.astype(jnp.float32) * (2.0 * math.pi / WIN))
    return jnp.where(inside, (values - average[:, :, None]) * taper[None, None, :], 0.0).astype(
        jnp.bfloat16
    )


def whiten(spectra):
    row_count = spectra.shape[0]
    grouped = spectra.reshape(row_count, 2, NB // SUB, SUB)
    power = jnp.sum(grouped * grouped, axis=(1, 3)) / SUB
    factor = lax.rsqrt(power + 1e-06)
    return (grouped * factor[:, None, :, None]).reshape(row_count, 2, NB).astype(jnp.bfloat16)


def spectra_of(shaped_rows):
    row_count = shaped_rows.shape[0]
    real_table, imag_table = quarter_table()
    table = jnp.asarray(np.concatenate([real_table, imag_table], axis=1))
    quarters = jnp.concatenate(
        [lax.slice_in_dim(shaped_rows, q * QUARTER, (q + 1) * QUARTER, axis=1) for q in range(4)], axis=0
    )
    parts = jnp.dot(quarters, table, preferred_element_type=jnp.float32).reshape(4, row_count, 2, NB)
    turn_real, turn_imag = (jnp.asarray(t)[:, None, :] for t in turns())
    real = jnp.sum(parts[:, :, 0] * turn_real - parts[:, :, 1] * turn_imag, axis=0)
    imag = jnp.sum(parts[:, :, 1] * turn_real + parts[:, :, 0] * turn_imag, axis=0)
    return whiten(jnp.concatenate([real, imag], axis=1))


def plain_body(raw, lengths, quality, assignment):
    my_index = lax.axis_index("chan")
    block_rows, window_count, sample_count = raw.shape
    total_channels = assignment.shape[0]
    my_quality = lax.dynamic_slice_in_dim(quality, my_index * block_rows, block_rows)
    shaped = prepare(raw, lengths)
    whitened = spectra_of(shaped.reshape(block_rows * window_count, sample_count)).reshape(
        block_rows, window_count, 2, NB
    )
    whitened = whitened * my_quality.astype(jnp.bfloat16)[:, None, None, None]
    panel = lax.all_to_all(whitened, "freq", split_axis=3, concat_axis=1, tiled=True)
    all_windows = panel.shape[1]
    gathered = lax.all_gather(panel, "chan", axis=0, tiled=True)
    positions = jnp.arange(total_channels, dtype=jnp.int32)
    place = (assignment[:, None] == positions[None, :]).astype(jnp.bfloat16)
    my_positions = my_index * block_rows + jnp.arange(block_rows, dtype=jnp.int32)
    my_place = (assignment[:, None] == my_positions[None, :]).astype(jnp.bfloat16)
    bins_here = gathered.shape[3]
    right = jnp.einsum("cwpb,cj->bpwj", gathered, place, preferred_element_type=jnp.float32)
    right = right.astype(jnp.bfloat16).reshape(bins_here, 2 * all_windows, total_channels)
    left = jnp.einsum("cwpb,ci->bipw", gathered, my_place, preferred_element_type=jnp.float32)
    left = left.astype(jnp.bfloat16)
    both = jnp.stack(
        [left, jnp.stack([left[:, :, 1], -left[:, :, 0]], axis=2)], axis=2
    ).reshape(bins_here, 2 * block_rows, 2 * all_windows)
    cross = jnp.einsum("bik,bkj->bij", both, right, preferred_element_type=jnp.float32)
    return (cross / all_windows).astype(jnp.bfloat16).reshape(bins_here, block_rows, 2, total_channels)


CHUNK = 128
DEPTH = 3072
MESH = pl.DeviceIdType.MESH


def spectra_kernel(raw_ref, length_ref, taper_ref, order_ref, table_ref, out_ref, rows):
    row_count = raw_ref.shape[0]

    @pl.when(pl.program_id(0) == 0)
    def _():
        rows[:, QUARTER // 128 * 128 :] = jnp.zeros(
            (4 * row_count, DEPTH - QUARTER // 128 * 128), jnp.bfloat16
        )
        taper = taper_ref[...]

        def prepare_rows(step, carry):
            first = pl.multiple_of(step * 16, 16)
            values = raw_ref[pl.ds(first, 16), :].astype(jnp.float32)
            valid = length_ref[pl.ds(first, 16), :]
            inside = lax.broadcasted_iota(jnp.int32, (16, WIN), 1) < valid
            kept = jnp.where(inside, values, 0.0)
            average = jnp.sum(kept, axis=1, keepdims=True) / valid.astype(jnp.float32)
            shaped = jnp.where(inside, (values - average) * taper, 0.0)
            for q in range(4):
                rows[pl.ds(pl.multiple_of(q * row_count + first, 16), 16), :QUARTER] = shaped[
                    :, q * QUARTER : (q + 1) * QUARTER
                ].astype(jnp.bfloat16)
            return carry

        lax.fori_loop(0, row_count // 16, prepare_rows, 0)

    parts = jnp.dot(rows[...], table_ref[0], preferred_element_type=jnp.float32)
    lanes = lax.broadcasted_iota(jnp.int32, (1, CHUNK), 1)
    group_row = lax.broadcasted_iota(jnp.int32, (CHUNK, CHUNK), 0) // SUB
    group_column = lax.broadcasted_iota(jnp.int32, (CHUNK, CHUNK), 1) // SUB
    real = jnp.zeros((row_count, CHUNK), jnp.float32)
    imag = jnp.zeros((row_count, CHUNK), jnp.float32)
    for q in range(4):
        a = parts[q * row_count : (q + 1) * row_count, :CHUNK]
        b = parts[q * row_count : (q + 1) * row_count, CHUNK:]
        turn = lax.rem(q * (K0 + lanes), 4)
        turn_real = (turn == 0).astype(jnp.float32) - (turn == 2).astype(jnp.float32)
        turn_imag = (turn == 3).astype(jnp.float32) - (turn == 1).astype(jnp.float32)
        real += a * turn_real - b * turn_imag
        imag += b * turn_real + a * turn_imag
    power = jnp.dot(
        real * real + imag * imag,
        (group_row == group_column).astype(jnp.float32),
        preferred_element_type=jnp.float32,
        precision=lax.Precision.HIGHEST,
    )
    factor = lax.rsqrt(power / SUB + 1e-06)
    for part, value in enumerate((real, imag)):
        out_ref[0, part * row_count : (part + 1) * row_count, :] = jnp.dot(
            order_ref[...], (value * factor).astype(jnp.bfloat16), preferred_element_type=jnp.float32
        ).astype(jnp.bfloat16)


def cross_kernel(
    own_ref,
    place_ref,
    out_ref,
    panel,
    right,
    local_sem,
    arrive,
    up_sem,
    down_sem,
    side_sem,
    core_sem,
    *,
    window_count,
):
    chunks = own_ref.shape[0]
    levels = panel.shape[0] // 4
    me = lax.axis_index("chan")
    core = lax.rem(me, 2)
    side = lax.rem(me // 2, 2)
    level = me // 4
    up, down = me + 4, me - 4
    beside = level * 4 + (1 - side) * 2 + core
    partner = level * 4 + side * 2 + (1 - core)
    has_up, has_down = level < levels - 1, level > 0

    barrier = pltpu.get_barrier_semaphore()

    def greet(target):
        pl.semaphore_signal(barrier, inc=1, device_id={"chan": target}, device_id_type=MESH)

    greet(beside)
    greet(partner)
    pl.when(has_up)(lambda: greet(up))
    pl.when(has_down)(lambda: greet(down))
    pl.semaphore_wait(barrier, 2 + has_up.astype(jnp.int32) + has_down.astype(jnp.int32))

    keep = pltpu.make_async_copy(own_ref, panel.at[me], local_sem)
    keep.start()

    def copy(kind, target, origin, chunk, mine=False):
        slot = {"up": origin // 4, "down": origin // 4, "side": origin // 4, "core": origin // 2}[kind]
        sems = {"up": up_sem, "down": down_sem, "side": side_sem, "core": core_sem}[kind]
        return pltpu.make_async_remote_copy(
            src_ref=own_ref.at[chunk] if mine else panel.at[origin, chunk],
            dst_ref=panel.at[origin, chunk],
            send_sem=sems.at[slot, chunk],
            recv_sem=arrive.at[origin, chunk],
            device_id={"chan": target},
            device_id_type=MESH,
        )

    def landed(origin, chunk):
        copy("core", partner, origin, chunk).wait_recv()

    def send_own(chunk, carry):
        copy("side", beside, me, chunk, True).start()
        pl.when(has_up)(lambda: copy("up", up, me, chunk, True).start())
        pl.when(has_down)(lambda: copy("down", down, me, chunk, True).start())
        copy("core", partner, me, chunk, True).start()
        return carry

    lax.fori_loop(0, chunks, send_own, 0)

    def from_side(distance, chunk):
        def pass_on(origin):
            landed(origin, chunk)
            copy("core", partner, origin, chunk).start()

        if distance == 0:
            pass_on(beside)
        else:
            pl.when(level >= distance)(lambda: pass_on(beside - 4 * distance))
            pl.when(level + distance < levels)(lambda: pass_on(beside + 4 * distance))

    def relay(distance, chunk):
        def below():
            origin = me - 4 * distance
            landed(origin, chunk)
            copy("side", beside, origin, chunk).start()
            pl.when(has_up)(lambda: copy("up", up, origin, chunk).start())
            copy("core", partner, origin, chunk).start()

        def above():
            origin = me + 4 * distance
            landed(origin, chunk)
            copy("side", beside, origin, chunk).start()
            pl.when(has_down)(lambda: copy("down", down, origin, chunk).start())
            copy("core", partner, origin, chunk).start()

        if distance < levels:
            pl.when(level >= distance)(below)
            pl.when(level + distance < levels)(above)
        from_side(distance - 1, chunk)

    depth = 2 * window_count
    devices = panel.shape[0]
    owner = lax.broadcasted_iota(jnp.int32, (128, 8 * depth), 0) // 16
    column = lax.broadcasted_iota(jnp.int32, (128, 8 * depth), 1) // depth
    mask = jnp.where(owner == column, 1.0 / window_count, 0.0).astype(jnp.bfloat16)
    target = lax.broadcasted_iota(jnp.int32, (16, 128), 0) // 2 + me * 8
    select = (lax.broadcasted_iota(jnp.int32, (16, 128), 1) == target).astype(jnp.float32).astype(jnp.bfloat16)
    spot = lax.broadcasted_iota(jnp.int32, (16, 8 * depth), 1)
    straight = lax.rem(lax.broadcasted_iota(jnp.int32, (16, 8 * depth), 0), 2) == 0
    first_half = lax.rem(spot, depth) < window_count

    def arrange(chunk):
        for pair in range(window_count):
            block = panel[:, chunk, pair * 16 : (pair + 1) * 16, :].reshape(devices * 16, CHUNK)
            turned = lax.dot_general(
                block, place_ref[...], (((0,), (0,)), ((), ())), preferred_element_type=jnp.float32
            )
            for half in range(2):
                right[pl.ds(pair * 2 + half, CHUNK, stride=depth), :] = turned[:, half * 128 : (half + 1) * 128]

    def multiply(chunk, first, last):
        for group in range(first, last):
            plain = right[group * 8 * depth : (group + 1) * 8 * depth, :].astype(jnp.bfloat16)
            left = lax.dot_general(select, plain, (((1,), (1,)), ((), ())), preferred_element_type=jnp.float32)
            later = pltpu.roll(left, 8 * depth - window_count, 1)
            earlier = pltpu.roll(left, window_count, 1)
            left = jnp.where(straight, left, jnp.where(first_half, later, -earlier)).astype(jnp.bfloat16)
            result = jnp.dot(
                jnp.concatenate([left] * 8, axis=0) * mask, plain, preferred_element_type=jnp.float32
            )
            row = pl.multiple_of((chunk * (CHUNK // 8) + group) * 128, 128)
            out_ref[pl.ds(row, 128), :] = result.astype(jnp.bfloat16)

    groups = CHUNK // 8

    def advance(step, carry):
        for distance in range(1, levels + 1):
            pl.when(step < chunks)(lambda distance=distance: relay(distance, step))

            @pl.when(step > 0)
            def _(distance=distance):
                if distance == 1:
                    arrange(step - 1)
                else:
                    multiply(
                        step - 1,
                        groups * (distance - 2) // (levels - 1),
                        groups * (distance - 1) // (levels - 1),
                    )

        @pl.when(step < chunks)
        def _():
            for z in range(levels):
                for y in range(2):
                    landed(z * 4 + y * 2 + (1 - core), step)

        return carry

    keep.wait()
    lax.fori_loop(0, chunks + 1, advance, 0)

    def finish(chunk, carry):
        for z in range(levels):
            line = z * 4 + side * 2 + core
            copy("side", beside, line, chunk).wait_send()
            copy("core", partner, line, chunk).wait_send()
            copy("core", partner, z * 4 + (1 - side) * 2 + core, chunk).wait_send()
            pl.when(jnp.logical_and(has_up, z <= level))(
                lambda line=line: copy("up", up, line, chunk).wait_send()
            )
            pl.when(jnp.logical_and(has_down, z >= level))(
                lambda line=line: copy("down", down, line, chunk).wait_send()
            )
        return carry

    lax.fori_loop(0, chunks, finish, 0)


def kernel_body(raw, lengths, quality, assignment):
    block_rows, window_count, _ = raw.shape
    row_count = block_rows * window_count
    total_channels = assignment.shape[0]
    devices = total_channels // block_rows
    chunks = NB // CHUNK
    real_table, imag_table = quarter_table()
    table = np.zeros((chunks, DEPTH, 2 * CHUNK), ml_dtypes.bfloat16)
    for chunk in range(chunks):
        table[chunk, :QUARTER, :CHUNK] = real_table[:, chunk * CHUNK : (chunk + 1) * CHUNK]
        table[chunk, :QUARTER, CHUNK:] = imag_table[:, chunk * CHUNK : (chunk + 1) * CHUNK]
    positions = np.arange(WIN, dtype=np.float32)
    taper = (0.5 - 0.5 * np.cos(positions * np.float32(2.0 * math.pi / WIN))).astype(np.float32)[None, :]
    flat = np.arange(row_count)
    shuffle = (
        (flat[:, None] // block_rows == flat[None, :] % window_count)
        & (flat[:, None] % block_rows == flat[None, :] // window_count)
    ).astype(ml_dtypes.bfloat16)

    def whole(shape):
        return pl.BlockSpec(shape, lambda j: (0,) * len(shape))

    own = pl.pallas_call(
        spectra_kernel,
        grid=(chunks,),
        in_specs=[
            whole((row_count, WIN)),
            whole((row_count, 1)),
            whole((1, WIN)),
            whole((row_count, row_count)),
            pl.BlockSpec((1, DEPTH, 2 * CHUNK), lambda j: (j, 0, 0)),
        ],
        out_specs=pl.BlockSpec((1, 2 * row_count, CHUNK), lambda j: (j, 0, 0)),
        out_shape=jax.ShapeDtypeStruct((chunks, 2 * row_count, CHUNK), jnp.bfloat16),
        scratch_shapes=[pltpu.VMEM((4 * row_count, DEPTH), jnp.bfloat16)],
        compiler_params=pltpu.CompilerParams(vmem_limit_bytes=48 * 2**20),
    )(
        raw.reshape(row_count, WIN),
        lengths.reshape(row_count, 1),
        jnp.asarray(taper),
        jnp.asarray(shuffle),
        jnp.asarray(table),
    )

    ordered = jnp.where(quality == 1, assignment, -1)
    spot = jnp.repeat(ordered.reshape(devices, 1, block_rows), 2, axis=1).reshape(-1)
    half = (np.arange(2 * total_channels) // block_rows) % 2
    columns = np.arange(2 * total_channels)
    place = jnp.logical_and(
        spot[:, None] == jnp.asarray(columns % total_channels)[None, :],
        jnp.asarray(half[:, None] == columns[None, :] // total_channels),
    ).astype(jnp.bfloat16)
    vmem = pl.BlockSpec(memory_space=pltpu.VMEM)
    cross = pl.pallas_call(
        functools.partial(cross_kernel, window_count=window_count),
        in_specs=[vmem] * 2,
        out_specs=vmem,
        out_shape=jax.ShapeDtypeStruct((NB * 2 * block_rows, total_channels), jnp.bfloat16),
        scratch_shapes=[
            pltpu.VMEM((devices, chunks, 2 * row_count, CHUNK), jnp.bfloat16),
            pltpu.VMEM((CHUNK * 2 * window_count, total_channels), jnp.float32),
            pltpu.SemaphoreType.DMA,
            pltpu.SemaphoreType.DMA((devices, chunks)),
            pltpu.SemaphoreType.DMA((devices // 4, chunks)),
            pltpu.SemaphoreType.DMA((devices // 4, chunks)),
            pltpu.SemaphoreType.DMA((devices // 4, chunks)),
            pltpu.SemaphoreType.DMA((devices // 2, chunks)),
        ],
        compiler_params=pltpu.CompilerParams(
            collective_id=0, has_side_effects=True, vmem_limit_bytes=48 * 2**20
        ),
    )(own, place)
    return cross.reshape(NB, block_rows, 2, total_channels)


def solution(mesh):
    ours = mesh.shape["freq"] == 1 and mesh.shape["chan"] == 16
    return jax.shard_map(
        kernel_body if ours else plain_body,
        mesh=mesh,
        in_specs=(
            P(("groups", "chan"), "freq", None),
            P(("groups", "chan"), "freq"),
            P("groups"),
            P("groups"),
        ),
        out_specs=P("freq", ("groups", "chan"), None, None),
        check_vma=False,
    )
```

```python
import functools
import math

import jax
import jax.numpy as jnp
import ml_dtypes
import numpy as np
from jax import lax
from jax.experimental import pallas as pl
from jax.experimental.pallas import tpu as pltpu
from jax.sharding import PartitionSpec as P

WIN = 12000
NB = 512
K0 = 6
SUB = 32
QUARTER = WIN // 4


def quarter_table():
    samples = np.arange(QUARTER, dtype=np.int64)
    bins = K0 + np.arange(NB, dtype=np.int64)
    residue = samples[:, None] * bins[None, :] % WIN
    angles = residue.astype(np.float32) * np.float32(2.0 * math.pi / WIN)
    real = np.cos(angles).astype(ml_dtypes.bfloat16)
    imag = (-np.sin(angles)).astype(ml_dtypes.bfloat16)
    return real, imag


def turns():
    power = (np.arange(4)[:, None] * (K0 + np.arange(NB))[None, :]) % 4
    real = np.array([1.0, 0.0, -1.0, 0.0], np.float32)[power]
    imag = np.array([0.0, -1.0, 0.0, 1.0], np.float32)[power]
    return real, imag


def prepare(raw_block, valid_lengths):
    positions = jnp.arange(WIN, dtype=jnp.int32)
    inside = positions[None, None, :] < valid_lengths[:, :, None]
    values = raw_block.astype(jnp.float32)
    kept = jnp.where(inside, values, 0.0)
    average = jnp.sum(kept, axis=-1) / valid_lengths.astype(jnp.float32)
    taper = 0.5 - 0.5 * jnp.cos(positions.astype(jnp.float32) * (2.0 * math.pi / WIN))
    return jnp.where(inside, (values - average[:, :, None]) * taper[None, None, :], 0.0).astype(
        jnp.bfloat16
    )


def whiten(spectra):
    row_count = spectra.shape[0]
    grouped = spectra.reshape(row_count, 2, NB // SUB, SUB)
    power = jnp.sum(grouped * grouped, axis=(1, 3)) / SUB
    factor = lax.rsqrt(power + 1e-06)
    return (grouped * factor[:, None, :, None]).reshape(row_count, 2, NB).astype(jnp.bfloat16)


def spectra_of(shaped_rows):
    row_count = shaped_rows.shape[0]
    real_table, imag_table = quarter_table()
    table = jnp.asarray(np.concatenate([real_table, imag_table], axis=1))
    quarters = jnp.concatenate(
        [lax.slice_in_dim(shaped_rows, q * QUARTER, (q + 1) * QUARTER, axis=1) for q in range(4)], axis=0
    )
    parts = jnp.dot(quarters, table, preferred_element_type=jnp.float32).reshape(4, row_count, 2, NB)
    turn_real, turn_imag = (jnp.asarray(t)[:, None, :] for t in turns())
    real = jnp.sum(parts[:, :, 0] * turn_real - parts[:, :, 1] * turn_imag, axis=0)
    imag = jnp.sum(parts[:, :, 1] * turn_real + parts[:, :, 0] * turn_imag, axis=0)
    return whiten(jnp.concatenate([real, imag], axis=1))


def plain_body(raw, lengths, quality, assignment):
    my_index = lax.axis_index("chan")
    block_rows, window_count, sample_count = raw.shape
    total_channels = assignment.shape[0]
    my_quality = lax.dynamic_slice_in_dim(quality, my_index * block_rows, block_rows)
    shaped = prepare(raw, lengths)
    whitened = spectra_of(shaped.reshape(block_rows * window_count, sample_count)).reshape(
        block_rows, window_count, 2, NB
    )
    whitened = whitened * my_quality.astype(jnp.bfloat16)[:, None, None, None]
    panel = lax.all_to_all(whitened, "freq", split_axis=3, concat_axis=1, tiled=True)
    all_windows = panel.shape[1]
    gathered = lax.all_gather(panel, "chan", axis=0, tiled=True)
    positions = jnp.arange(total_channels, dtype=jnp.int32)
    place = (assignment[:, None] == positions[None, :]).astype(jnp.bfloat16)
    my_positions = my_index * block_rows + jnp.arange(block_rows, dtype=jnp.int32)
    my_place = (assignment[:, None] == my_positions[None, :]).astype(jnp.bfloat16)
    bins_here = gathered.shape[3]
    right = jnp.einsum("cwpb,cj->bpwj", gathered, place, preferred_element_type=jnp.float32)
    right = right.astype(jnp.bfloat16).reshape(bins_here, 2 * all_windows, total_channels)
    left = jnp.einsum("cwpb,ci->bipw", gathered, my_place, preferred_element_type=jnp.float32)
    left = left.astype(jnp.bfloat16)
    both = jnp.stack(
        [left, jnp.stack([left[:, :, 1], -left[:, :, 0]], axis=2)], axis=2
    ).reshape(bins_here, 2 * block_rows, 2 * all_windows)
    cross = jnp.einsum("bik,bkj->bij", both, right, preferred_element_type=jnp.float32)
    return (cross / all_windows).astype(jnp.bfloat16).reshape(bins_here, block_rows, 2, total_channels)


CHUNK = 128
DEPTH = 3072
MESH = pl.DeviceIdType.MESH


def spectra_kernel(raw_ref, length_ref, taper_ref, order_ref, table_ref, out_ref, rows):
    row_count = raw_ref.shape[0]

    @pl.when(pl.program_id(0) == 0)
    def _():
        rows[:, QUARTER // 128 * 128 :] = jnp.zeros(
            (4 * row_count, DEPTH - QUARTER // 128 * 128), jnp.bfloat16
        )
        taper = taper_ref[...]

        def prepare_rows(step, carry):
            first = pl.multiple_of(step * 16, 16)
            values = raw_ref[pl.ds(first, 16), :].astype(jnp.float32)
            valid = length_ref[pl.ds(first, 16), :]
            inside = lax.broadcasted_iota(jnp.int32, (16, WIN), 1) < valid
            kept = jnp.where(inside, values, 0.0)
            average = jnp.sum(kept, axis=1, keepdims=True) / valid.astype(jnp.float32)
            shaped = jnp.where(inside, (values - average) * taper, 0.0)
            for q in range(4):
                rows[pl.ds(pl.multiple_of(q * row_count + first, 16), 16), :QUARTER] = shaped[
                    :, q * QUARTER : (q + 1) * QUARTER
                ].astype(jnp.bfloat16)
            return carry

        lax.fori_loop(0, row_count // 16, prepare_rows, 0)

    parts = jnp.dot(rows[...], table_ref[0], preferred_element_type=jnp.float32)
    lanes = lax.broadcasted_iota(jnp.int32, (1, CHUNK), 1)
    group_row = lax.broadcasted_iota(jnp.int32, (CHUNK, CHUNK), 0) // SUB
    group_column = lax.broadcasted_iota(jnp.int32, (CHUNK, CHUNK), 1) // SUB
    real = jnp.zeros((row_count, CHUNK), jnp.float32)
    imag = jnp.zeros((row_count, CHUNK), jnp.float32)
    for q in range(4):
        a = parts[q * row_count : (q + 1) * row_count, :CHUNK]
        b = parts[q * row_count : (q + 1) * row_count, CHUNK:]
        turn = lax.rem(q * (K0 + lanes), 4)
        turn_real = (turn == 0).astype(jnp.float32) - (turn == 2).astype(jnp.float32)
        turn_imag = (turn == 3).astype(jnp.float32) - (turn == 1).astype(jnp.float32)
        real += a * turn_real - b * turn_imag
        imag += b * turn_real + a * turn_imag
    power = jnp.dot(
        real * real + imag * imag,
        (group_row == group_column).astype(jnp.float32),
        preferred_element_type=jnp.float32,
        precision=lax.Precision.HIGHEST,
    )
    factor = lax.rsqrt(power / SUB + 1e-06)
    for part, value in enumerate((real, imag)):
        out_ref[0, part * row_count : (part + 1) * row_count, :] = jnp.dot(
            order_ref[...], (value * factor).astype(jnp.bfloat16), preferred_element_type=jnp.float32
        ).astype(jnp.bfloat16)


def cross_kernel(
    own_ref,
    place_ref,
    out_ref,
    panel,
    right,
    local_sem,
    arrive,
    up_sem,
    down_sem,
    side_sem,
    core_sem,
    *,
    window_count,
):
    chunks = own_ref.shape[0]
    levels = panel.shape[0] // 4
    me = lax.axis_index("chan")
    core = lax.rem(me, 2)
    side = lax.rem(me // 2, 2)
    level = me // 4
    up, down = me + 4, me - 4
    beside = level * 4 + (1 - side) * 2 + core
    partner = level * 4 + side * 2 + (1 - core)
    has_up, has_down = level < levels - 1, level > 0

    barrier = pltpu.get_barrier_semaphore()

    def greet(target):
        pl.semaphore_signal(barrier, inc=1, device_id={"chan": target}, device_id_type=MESH)

    greet(beside)
    greet(partner)
    pl.when(has_up)(lambda: greet(up))
    pl.when(has_down)(lambda: greet(down))
    pl.semaphore_wait(barrier, 2 + has_up.astype(jnp.int32) + has_down.astype(jnp.int32))

    keep = pltpu.make_async_copy(own_ref, panel.at[me], local_sem)
    keep.start()

    def copy(kind, target, origin, chunk, mine=False):
        slot = {"up": origin // 4, "down": origin // 4, "side": origin // 4, "core": origin // 2}[kind]
        sems = {"up": up_sem, "down": down_sem, "side": side_sem, "core": core_sem}[kind]
        return pltpu.make_async_remote_copy(
            src_ref=own_ref.at[chunk] if mine else panel.at[origin, chunk],
            dst_ref=panel.at[origin, chunk],
            send_sem=sems.at[slot, chunk],
            recv_sem=arrive.at[origin, chunk],
            device_id={"chan": target},
            device_id_type=MESH,
        )

    def landed(origin, chunk):
        copy("core", partner, origin, chunk).wait_recv()

    def send_own(chunk, carry):
        copy("side", beside, me, chunk, True).start()
        pl.when(has_up)(lambda: copy("up", up, me, chunk, True).start())
        pl.when(has_down)(lambda: copy("down", down, me, chunk, True).start())
        copy("core", partner, me, chunk, True).start()
        return carry

    lax.fori_loop(0, chunks, send_own, 0)

    def from_side(distance, chunk):
        def pass_on(origin):
            landed(origin, chunk)
            copy("core", partner, origin, chunk).start()

        if distance == 0:
            pass_on(beside)
        else:
            pl.when(level >= distance)(lambda: pass_on(beside - 4 * distance))
            pl.when(level + distance < levels)(lambda: pass_on(beside + 4 * distance))

    def relay(distance, chunk):
        def below():
            origin = me - 4 * distance
            landed(origin, chunk)
            copy("side", beside, origin, chunk).start()
            pl.when(has_up)(lambda: copy("up", up, origin, chunk).start())
            copy("core", partner, origin, chunk).start()

        def above():
            origin = me + 4 * distance
            landed(origin, chunk)
            copy("side", beside, origin, chunk).start()
            pl.when(has_down)(lambda: copy("down", down, origin, chunk).start())
            copy("core", partner, origin, chunk).start()

        if distance < levels:
            pl.when(level >= distance)(below)
            pl.when(level + distance < levels)(above)
        from_side(distance - 1, chunk)

    depth = 2 * window_count
    devices = panel.shape[0]
    owner = lax.broadcasted_iota(jnp.int32, (128, 8 * depth), 0) // 16
    column = lax.broadcasted_iota(jnp.int32, (128, 8 * depth), 1) // depth
    mask = jnp.where(owner == column, 1.0 / window_count, 0.0).astype(jnp.bfloat16)
    target = lax.broadcasted_iota(jnp.int32, (16, 128), 0) // 2 + me * 8
    select = (lax.broadcasted_iota(jnp.int32, (16, 128), 1) == target).astype(jnp.float32).astype(jnp.bfloat16)
    spot = lax.broadcasted_iota(jnp.int32, (16, 8 * depth), 1)
    straight = lax.rem(lax.broadcasted_iota(jnp.int32, (16, 8 * depth), 0), 2) == 0
    first_half = lax.rem(spot, depth) < window_count

    def arrange(chunk):
        for pair in range(window_count):
            block = panel[:, chunk, pair * 16 : (pair + 1) * 16, :].reshape(devices * 16, CHUNK)
            turned = lax.dot_general(
                block, place_ref[...], (((0,), (0,)), ((), ())), preferred_element_type=jnp.float32
            )
            for half in range(2):
                right[pl.ds(pair * 2 + half, CHUNK, stride=depth), :] = turned[:, half * 128 : (half + 1) * 128]

    def multiply(chunk, first, last):
        for group in range(first, last):
            plain = right[group * 8 * depth : (group + 1) * 8 * depth, :].astype(jnp.bfloat16)
            left = lax.dot_general(select, plain, (((1,), (1,)), ((), ())), preferred_element_type=jnp.float32)
            later = pltpu.roll(left, 8 * depth - window_count, 1)
            earlier = pltpu.roll(left, window_count, 1)
            left = jnp.where(straight, left, jnp.where(first_half, later, -earlier)).astype(jnp.bfloat16)
            result = jnp.dot(
                jnp.concatenate([left] * 8, axis=0) * mask, plain, preferred_element_type=jnp.float32
            )
            row = pl.multiple_of((chunk * (CHUNK // 8) + group) * 128, 128)
            out_ref[pl.ds(row, 128), :] = result.astype(jnp.bfloat16)

    groups = CHUNK // 8

    def advance(step, carry):
        for distance in range(1, levels + 1):
            chunk = step - distance + 1
            pl.when(jnp.logical_and(chunk >= 0, chunk < chunks))(
                lambda distance=distance, chunk=chunk: relay(distance, chunk)
            )

        @pl.when(step >= levels)
        def _():
            chunk = step - levels
            for z in range(levels):
                for y in range(2):
                    landed(z * 4 + y * 2 + (1 - core), chunk)
            arrange(chunk)
            multiply(chunk, 0, groups)

        return carry

    keep.wait()
    lax.fori_loop(0, chunks + levels, advance, 0)

    def finish(chunk, carry):
        for z in range(levels):
            line = z * 4 + side * 2 + core
            copy("side", beside, line, chunk).wait_send()
            copy("core", partner, line, chunk).wait_send()
            copy("core", partner, z * 4 + (1 - side) * 2 + core, chunk).wait_send()
            pl.when(jnp.logical_and(has_up, z <= level))(
                lambda line=line: copy("up", up, line, chunk).wait_send()
            )
            pl.when(jnp.logical_and(has_down, z >= level))(
                lambda line=line: copy("down", down, line, chunk).wait_send()
            )
        return carry

    lax.fori_loop(0, chunks, finish, 0)


def kernel_body(raw, lengths, quality, assignment):
    block_rows, window_count, _ = raw.shape
    row_count = block_rows * window_count
    total_channels = assignment.shape[0]
    devices = total_channels // block_rows
    chunks = NB // CHUNK
    real_table, imag_table = quarter_table()
    table = np.zeros((chunks, DEPTH, 2 * CHUNK), ml_dtypes.bfloat16)
    for chunk in range(chunks):
        table[chunk, :QUARTER, :CHUNK] = real_table[:, chunk * CHUNK : (chunk + 1) * CHUNK]
        table[chunk, :QUARTER, CHUNK:] = imag_table[:, chunk * CHUNK : (chunk + 1) * CHUNK]
    positions = np.arange(WIN, dtype=np.float32)
    taper = (0.5 - 0.5 * np.cos(positions * np.float32(2.0 * math.pi / WIN))).astype(np.float32)[None, :]
    flat = np.arange(row_count)
    shuffle = (
        (flat[:, None] // block_rows == flat[None, :] % window_count)
        & (flat[:, None] % block_rows == flat[None, :] // window_count)
    ).astype(ml_dtypes.bfloat16)

    def whole(shape):
        return pl.BlockSpec(shape, lambda j: (0,) * len(shape))

    own = pl.pallas_call(
        spectra_kernel,
        grid=(chunks,),
        in_specs=[
            whole((row_count, WIN)),
            whole((row_count, 1)),
            whole((1, WIN)),
            whole((row_count, row_count)),
            pl.BlockSpec((1, DEPTH, 2 * CHUNK), lambda j: (j, 0, 0)),
        ],
        out_specs=pl.BlockSpec((1, 2 * row_count, CHUNK), lambda j: (j, 0, 0)),
        out_shape=jax.ShapeDtypeStruct((chunks, 2 * row_count, CHUNK), jnp.bfloat16),
        scratch_shapes=[pltpu.VMEM((4 * row_count, DEPTH), jnp.bfloat16)],
        compiler_params=pltpu.CompilerParams(vmem_limit_bytes=48 * 2**20),
    )(
        raw.reshape(row_count, WIN),
        lengths.reshape(row_count, 1),
        jnp.asarray(taper),
        jnp.asarray(shuffle),
        jnp.asarray(table),
    )

    ordered = jnp.where(quality == 1, assignment, -1)
    spot = jnp.repeat(ordered.reshape(devices, 1, block_rows), 2, axis=1).reshape(-1)
    half = (np.arange(2 * total_channels) // block_rows) % 2
    columns = np.arange(2 * total_channels)
    place = jnp.logical_and(
        spot[:, None] == jnp.asarray(columns % total_channels)[None, :],
        jnp.asarray(half[:, None] == columns[None, :] // total_channels),
    ).astype(jnp.bfloat16)
    vmem = pl.BlockSpec(memory_space=pltpu.VMEM)
    cross = pl.pallas_call(
        functools.partial(cross_kernel, window_count=window_count),
        in_specs=[vmem] * 2,
        out_specs=vmem,
        out_shape=jax.ShapeDtypeStruct((NB * 2 * block_rows, total_channels), jnp.bfloat16),
        scratch_shapes=[
            pltpu.VMEM((devices, chunks, 2 * row_count, CHUNK), jnp.bfloat16),
            pltpu.VMEM((CHUNK * 2 * window_count, total_channels), jnp.float32),
            pltpu.SemaphoreType.DMA,
            pltpu.SemaphoreType.DMA((devices, chunks)),
            pltpu.SemaphoreType.DMA((devices // 4, chunks)),
            pltpu.SemaphoreType.DMA((devices // 4, chunks)),
            pltpu.SemaphoreType.DMA((devices // 4, chunks)),
            pltpu.SemaphoreType.DMA((devices // 2, chunks)),
        ],
        compiler_params=pltpu.CompilerParams(
            collective_id=0, has_side_effects=True, vmem_limit_bytes=48 * 2**20
        ),
    )(own, place)
    return cross.reshape(NB, block_rows, 2, total_channels)


def solution(mesh):
    ours = mesh.shape["freq"] == 1 and mesh.shape["chan"] == 16
    return jax.shard_map(
        kernel_body if ours else plain_body,
        mesh=mesh,
        in_specs=(
            P(("groups", "chan"), "freq", None),
            P(("groups", "chan"), "freq"),
            P("groups"),
            P("groups"),
        ),
        out_specs=P("freq", ("groups", "chan"), None, None),
        check_vma=False,
    )
```
